32 devices in a mesh: leaf: 32 (over z, y, x, core).
Axes of the slice: x: 2, y: 2, z: 4, core: 2. Of those that a mesh axis runs over, the one named last changes fastest.
Arguments:
- points: bfloat16 [64, 131072], P(None, 'leaf'), may hold values from -0.8 to 0.8
- leaf_order: int32 [131072], P('leaf'), may hold values from 0 to 4095, as said below
- near_pairs: int32 [256, 4], P('leaf'), may hold values from -1 to 255, as said below
- solution: float32 [64, 131072], P(None, 'leaf'), may hold values from -6 to 6
- residual: float32 [64, 131072], P(None, 'leaf'), may hold values from -44 to 44
- direction: float32 [64, 131072], P(None, 'leaf'), may hold values from -44 to 44
- skeleton_basis: bfloat16 [256, 131072], P(None, 'leaf'), may hold values from -0.1875 to 0.1875
- transfers: float32 [160, 256, 256], P('leaf'), may hold values from -0.375 to 0.375
- couplings: float32 [6, 256, 256], replicated, may hold values from -0.375 to 0.375
Outputs:
- new_solution: float32 [64, 131072], P(None, 'leaf')
- new_residual: float32 [64, 131072], P(None, 'leaf')
- new_direction: float32 [64, 131072], P(None, 'leaf')
The draws below stay inside these ranges and needn't reach their ends.
Inputs may be any that keep to these rules, and one draw needn't show every extreme that they name: `leaf_order`: the entries of each slab's 4096 positions are a permutation of 0 to 4095. `near_pairs`: row a lists 4 different later leaves: the first is always a + 1, the others lie among a + 2 to a + 8; -1 stands where that leaf would lie past the last leaf.
All inputs are finite; a program needn't handle non-finite values.
Results may differ from the reference program's by a relative error of at most 0.0034.
The reference program's roundings to bfloat16 on the way count: a program that leaves them out, or rounds other values in their place, can miss the bound.
Values may be sent and summed in bfloat16 or wider, within the bound.
A program may use at most 128 MiB of HBM per device.

```python
import jax
import jax.numpy as jnp
from jax import lax

DIM = 64
LEAF = 512
RANK = 256
NRHS = 64
LEAF_DEV = 8
NPAIR = 4
LEVELS = 5
PTS_DEV = 4096
LEAVES = 256
NPTS = 131072
STACK = 160
N_LEAF = 32


def order_helper(key):
    keys = jax.random.split(jax.random.fold_in(key, 7), NPTS // PTS_DEV)
    perms = jax.vmap(lambda one_key: jax.random.permutation(one_key, PTS_DEV))(keys)
    return perms.astype(jnp.int32)


def draw_leaf_order(key, part):
    return order_helper(key).reshape(-1)


def draw_points(key, part):
    perms = order_helper(key)
    inverse = jnp.argsort(perms, axis=1).astype(jnp.int32)
    blocks = jnp.arange(NPTS // PTS_DEV, dtype=jnp.int32)[:, None] * PTS_DEV
    leaf_ids = ((blocks + inverse) // LEAF).reshape(-1)
    salted = jax.random.fold_in(key, 9)
    center_key, noise_key = jax.random.split(salted, 2)
    centers = jnp.clip(jax.random.normal(center_key, (DIM, LEAVES), jnp.float32), -5.0, 5.0) / 32.0
    noise = jnp.clip(jax.random.normal(noise_key, (DIM, NPTS), jnp.float32), -5.0, 5.0) / 8.0
    coords = jnp.take(centers, leaf_ids, axis=1) + noise
    return coords.astype(jnp.bfloat16)


def draw_near_pairs(key, part):
    keys = jax.random.split(jax.random.fold_in(key, 3), LEAVES)
    perms = jax.vmap(lambda one_key: jax.random.permutation(one_key, LEAF_DEV - 1))(keys).astype(jnp.int32)
    offsets = jnp.concatenate([jnp.ones((LEAVES, 1), jnp.int32), perms[:, :NPAIR - 1] + 2], axis=1)
    partner = jnp.arange(LEAVES, dtype=jnp.int32)[:, None] + offsets
    return jnp.where(partner < LEAVES, partner, -1).astype(jnp.int32)


def state_draw(key, salt):
    salted = jax.random.fold_in(key, salt)
    value_key, spread_key, column_key = jax.random.split(salted, 3)
    where_at = jnp.arange(NPTS, dtype=jnp.float32) / NPTS
    ramp = jnp.sqrt(1.0 + 2.0 * where_at)
    spread = jnp.exp(jax.random.uniform(spread_key, (NPTS,), jnp.float32, -1.15, 1.15))
    columns = jnp.exp(jax.random.uniform(column_key, (NRHS, 1), jnp.float32, -0.55, 0.55))
    values = jnp.clip(jax.random.normal(value_key, (NRHS, NPTS), jnp.float32), -4.5, 4.5)
    return (values * columns * (ramp * spread)[None, :]).astype(jnp.float32)


def coherent_draw(key, salt):
    salted = jax.random.fold_in(key, salt)
    value_key, spread_key, column_key, level_key, sign_key = jax.random.split(salted, 5)
    where_at = jnp.arange(NPTS, dtype=jnp.float32) / NPTS
    ramp = jnp.sqrt(1.0 + 2.0 * where_at)
    spread = jnp.exp(jax.random.uniform(spread_key, (NPTS,), jnp.float32, -1.15, 1.15))
    columns = jnp.exp(jax.random.uniform(column_key, (NRHS, 1), jnp.float32, -0.55, 0.55))
    levels_per_leaf = jax.random.uniform(level_key, (NRHS, LEAVES), jnp.float32, 0.5, 1.5)
    signs = (jax.random.randint(sign_key, (NRHS, 1), 0, 2) * 2 - 1).astype(jnp.float32)
    leaf_part = jnp.repeat(levels_per_leaf, LEAF, axis=1) * signs
    own_part = jnp.clip(jax.random.normal(value_key, (NRHS, NPTS), jnp.float32), -4.5, 4.5)
    values = 0.8 * own_part + 0.6 * leaf_part
    return (values * columns * (ramp * spread)[None, :]).astype(jnp.float32)


def draw_residual(key, part):
    return state_draw(key, 21)


def draw_direction(key, part):
    mixed = 0.8 * state_draw(key, 21) + 0.6 * coherent_draw(key, 22)
    return jnp.clip(mixed, -44.0, 44.0).astype(jnp.float32)


def levels(stream_key, extent, pieces, smallest, largest):
    def one(position, blocks):
        heights = jax.random.uniform(jax.random.fold_in(jax.random.fold_in(stream_key, 6), position), (blocks,), jnp.float32, smallest / len(pieces), largest / len(pieces))
        return jnp.repeat(jnp.exp(heights), extent[position] // blocks).reshape((-1,) + (1,) * (len(extent) - position - 1))

    level = one(*pieces[0])
    for cut in pieces[1:]:
        level = level * one(*cut)
    return level


def bell_draw(own_key, dims, width, bound, shards=(), held_as=jnp.bfloat16):
    result = jax.random.normal(own_key, dims, jnp.float32) * width
    if len(shards) > 0:
        result = levels(own_key, dims, shards, -0.22, 0.18) * result
    return jnp.clip(result, min=-bound, max=bound).astype(held_as)


def setup_inputs(seed: int = 0) -> dict:
    key_list = jax.random.split(jax.random.key(seed), 10)
    points = draw_points(jax.random.fold_in(key_list[9], 71), 0)
    leaf_order = draw_leaf_order(jax.random.fold_in(key_list[9], 71), 0)
    near_pairs = draw_near_pairs(jax.random.fold_in(key_list[9], 71), 0)
    solution = bell_draw(key_list[3], (NRHS, NPTS), 1.0, 6.0, ((1, 32),), jnp.float32)
    residual = draw_residual(jax.random.fold_in(key_list[9], 71), 0)
    direction = draw_direction(jax.random.fold_in(key_list[9], 71), 0)
    skeleton_basis = bell_draw(key_list[6], (RANK, NPTS), (PTS_DEV // 4) ** -0.5, 0.1875, ((1, 32),))
    transfers = bell_draw(key_list[7], (STACK, RANK, RANK), RANK ** -0.5, 0.375, ((0, 32),), jnp.float32)
    couplings = bell_draw(key_list[8], (LEVELS + 1, RANK, RANK), RANK ** -0.5, 0.375, (), jnp.float32)
    return {"points": points, "leaf_order": leaf_order, "near_pairs": near_pairs, "solution": solution, "residual": residual, "direction": direction, "skeleton_basis": skeleton_basis, "transfers": transfers, "couplings": couplings}


SHARPNESS = 2.0
EPSILON = 1e-6
HIGHEST = lax.Precision.HIGHEST


def couple(level_total, weights):
    halfway = jnp.matmul(level_total, weights, precision=HIGHEST)
    return jnp.matmul(halfway, jnp.swapaxes(weights, -1, -2), precision=HIGHEST)


def near_field(tree_points, p_half, near_pairs):
    leaf_points = tree_points.reshape(DIM, LEAVES, LEAF).astype(jnp.float32)
    leaf_values = p_half.reshape(NRHS, LEAVES, LEAF).astype(jnp.float32)
    squares = jnp.sum(leaf_points * leaf_points, axis=0)
    is_valid = near_pairs >= 0
    partner_ids = jnp.where(is_valid, near_pairs, 0).astype(jnp.int32)
    valid_int = is_valid.astype(jnp.int32)
    pair_totals = jnp.sum(valid_int, axis=1) + jnp.zeros((LEAVES,), jnp.int32).at[partner_ids.reshape(-1)].add(valid_int.reshape(-1))
    valid_float = is_valid.astype(jnp.float32)

    def visit_leaf(accum, leaf_index):
        row_ids = lax.dynamic_index_in_dim(partner_ids, leaf_index, 0, keepdims=False)
        row_weights = lax.dynamic_index_in_dim(valid_float, leaf_index, 0, keepdims=False)
        own_total = lax.dynamic_index_in_dim(pair_totals, leaf_index, 0, keepdims=False)
        others = jnp.concatenate([leaf_index[None].astype(jnp.int32), row_ids])
        source_weight = jnp.concatenate([(1 + own_total).astype(jnp.float32)[None], row_weights])
        other_weight = jnp.concatenate([jnp.zeros((1,), jnp.float32), row_weights])
        source_pts = lax.dynamic_index_in_dim(leaf_points, leaf_index, 1, keepdims=False)
        source_sq = lax.dynamic_index_in_dim(squares, leaf_index, 0, keepdims=False)
        source_val = lax.dynamic_index_in_dim(leaf_values, leaf_index, 1, keepdims=False)
        other_pts = jnp.take(leaf_points, others, axis=1)
        other_sq = jnp.take(squares, others, axis=0)
        other_val = jnp.take(leaf_values, others, axis=1)
        cross_dot = jnp.einsum("dk,dnj->nkj", source_pts, other_pts)
        distance = source_sq[None, :, None] + other_sq[:, None, :] - 2.0 * cross_dot
        kernel_tile = lax.optimization_barrier(jnp.exp(-SHARPNESS * distance).astype(jnp.bfloat16)).astype(jnp.float32)
        to_source = jnp.einsum("nkj,rnj->nrk", kernel_tile, other_val)
        to_source = jnp.sum(to_source * source_weight[:, None, None], axis=0)
        to_other = jnp.einsum("nkj,rk->rnj", kernel_tile, source_val) * other_weight[None, :, None]
        accum = accum.at[:, leaf_index, :].add(to_source)
        accum = accum.at[:, others, :].add(to_other)
        return accum, None

    start = jnp.zeros((NRHS, LEAVES, LEAF), jnp.float32)
    accum = lax.scan(visit_leaf, start, jnp.arange(LEAVES, dtype=jnp.int32))[0]
    return accum.reshape(NRHS, NPTS)


def far_field(p_half, skeleton_basis, transfers, couplings):
    slab_values = p_half.reshape(NRHS, N_LEAF, PTS_DEV).astype(jnp.float32)
    slab_basis = skeleton_basis.reshape(RANK, N_LEAF, PTS_DEV).astype(jnp.float32)
    slab_transfers = transfers.reshape(N_LEAF, LEVELS, RANK, RANK)
    level_skel = jnp.einsum("rsi,csi->src", slab_values, slab_basis)
    skeletons = [level_skel]
    for level_idx in range(LEVELS):
        level_skel = jnp.einsum("src,scd->srd", level_skel, slab_transfers[:, level_idx], precision=HIGHEST)
        skeletons.append(level_skel)
    top_total = jnp.sum(skeletons[LEVELS], axis=0)
    descent = jnp.broadcast_to(couple(top_total, couplings[LEVELS]), (N_LEAF, NRHS, RANK))
    for level_idx in reversed(range(LEVELS)):
        group = 2 ** (level_idx + 1)
        grouped = jnp.sum(skeletons[level_idx].reshape(N_LEAF // group, group, NRHS, RANK), axis=1)
        level_total = jnp.repeat(grouped, group, axis=0)
        descent = jnp.einsum("src,sdc->srd", descent, slab_transfers[:, level_idx], precision=HIGHEST) + couple(level_total, couplings[level_idx])
    descent_half = lax.optimization_barrier(descent.astype(jnp.bfloat16)).astype(jnp.float32)
    far = jnp.einsum("src,csi->rsi", descent_half, slab_basis)
    return far.reshape(NRHS, NPTS)


def reference(points, leaf_order, near_pairs, solution, residual, direction, skeleton_basis, transfers, couplings):
    positions = jnp.arange(NPTS, dtype=jnp.int32)
    source_cols = ((positions // PTS_DEV) * PTS_DEV + leaf_order).astype(jnp.int32)
    tree_points = jnp.take(points, source_cols, axis=1)
    p_half = lax.optimization_barrier(direction.astype(jnp.bfloat16))
    near = near_field(tree_points, p_half, near_pairs)
    far = far_field(p_half, skeleton_basis, transfers, couplings)
    image = direction + near + far
    old_norm = jnp.sum(residual * residual, axis=1)
    curve_sum = jnp.sum(direction * image, axis=1)
    step_size = old_norm / (curve_sum + EPSILON)
    new_solution = solution + step_size[:, None] * direction
    new_residual = residual - step_size[:, None] * image
    new_norm = jnp.sum(new_residual * new_residual, axis=1)
    ratio = new_norm / (old_norm + EPSILON)
    new_direction = new_residual + ratio[:, None] * direction
    return new_solution, new_residual, new_direction
```

```python
import functools
import math

import jax
import jax.numpy as jnp
from jax import lax
from jax.experimental import pallas as pl
from jax.experimental.pallas import tpu as pltpu
from jax.sharding import PartitionSpec as P

SHARPNESS = 2.0
EPSILON = 1e-06
HIGHEST = lax.Precision.HIGHEST
MESH = pl.DeviceIdType.MESH
LANES = 128
EXTRA = 16
GROUP = 8
VMEM_LIMIT = 56 * 1024 * 1024
NT = (((1,), (1,)), ((), ()))


def shifted(x, axis, by, wrap=False):
    peers = lax.axis_size(axis)
    pairs = [(i, (i + by) % peers) for i in range(peers) if wrap or 0 <= i + by < peers]
    return lax.ppermute(x, axis, pairs)


def swapped(x, axis, bit):
    count = lax.axis_size(axis)
    return lax.ppermute(x, axis, [(i, i ^ (1 << bit)) for i in range(count)])


def arrange_kernel(points_ref, order_ref, direction_ref, stack_ref, turned_ref, tall):
    coords, slab = points_ref.shape
    width = order_ref.shape[1]
    chunks = slab // LANES

    @pl.when(pl.program_id(0) == 0)
    def _():
        for h in range(chunks):
            tall[h * coords : (h + 1) * coords, :] = points_ref[:, h * LANES : (h + 1) * LANES]

    order = order_ref[...]
    high = order // LANES
    low = order - high * LANES
    rows = lax.broadcasted_iota(jnp.int32, (LANES, width), 0)
    onehot = jnp.where(rows == low, 1.0, 0.0).astype(jnp.bfloat16)
    picked = jnp.zeros((coords, width), jnp.float32)
    step = 4
    for c in range(0, chunks, step):
        part = jnp.dot(
            tall[c * coords : (c + step) * coords, :], onehot, preferred_element_type=jnp.float32
        )
        for h in range(step):
            picked = jnp.where(high == c + h, part[h * coords : (h + 1) * coords], picked)
    half = -0.5 * jnp.sum(picked * picked, axis=0, keepdims=True)
    first = half.astype(jnp.bfloat16).astype(jnp.float32)
    second = (half - first).astype(jnp.bfloat16).astype(jnp.float32)
    third = (half - first - second).astype(jnp.bfloat16).astype(jnp.float32)

    def extra(height, at_parts, at_ones):
        row = lax.broadcasted_iota(jnp.int32, (height, width), 0)
        out = jnp.where((row >= at_ones) & (row < at_ones + 3), 1.0, 0.0)
        for i, piece in enumerate((first, second, third)):
            out = jnp.where(row == at_parts + i, piece, out)
        return out

    stack_ref[0:coords, :] = picked.astype(jnp.bfloat16)
    stack_ref[coords : coords + EXTRA, :] = extra(EXTRA, 0, 3).astype(jnp.bfloat16)
    stack_ref[coords + EXTRA :, :] = direction_ref[...].astype(jnp.bfloat16)
    wide = jnp.concatenate([picked, extra(LANES - coords, 3, 0)], axis=0)
    turned_ref[...] = wide.T.astype(jnp.bfloat16)


def arrange(points, leaf_order, direction, leaf_size):
    coords, slab = points.shape
    rhs = direction.shape[0]
    height = coords + EXTRA + rhs
    return pl.pallas_call(
        arrange_kernel,
        grid=(slab // leaf_size,),
        in_specs=[
            pl.BlockSpec((coords, slab), lambda j: (0, 0)),
            pl.BlockSpec((1, leaf_size), lambda j: (0, j)),
            pl.BlockSpec((rhs, leaf_size), lambda j: (0, j)),
        ],
        out_specs=[
            pl.BlockSpec((height, leaf_size), lambda j: (0, j)),
            pl.BlockSpec((leaf_size, LANES), lambda j: (j, 0)),
        ],
        out_shape=[
            jax.ShapeDtypeStruct((height, slab), jnp.bfloat16),
            jax.ShapeDtypeStruct((slab, LANES), jnp.bfloat16),
        ],
        scratch_shapes=[pltpu.VMEM((slab // LANES * coords, LANES), jnp.bfloat16)],
        compiler_params=pltpu.CompilerParams(vmem_limit_bytes=VMEM_LIMIT),
        cost_estimate=pl.CostEstimate(
            flops=2 * coords * slab * slab, bytes_accessed=5 << 20, transcendentals=0
        ),
        name="arrange",
    )(points, leaf_order.reshape(1, slab), direction)


def rise_kernel(direction_ref, basis_ref, transfers_ref, skel_ref):
    value = lax.dot_general(
        direction_ref[...].astype(jnp.bfloat16),
        basis_ref[...],
        NT,
        preferred_element_type=jnp.float32,
    )
    skel_ref[0] = value
    for k in range(transfers_ref.shape[0]):
        value = jnp.dot(
            value, transfers_ref[k], precision=HIGHEST, preferred_element_type=jnp.float32
        )
        skel_ref[k + 1] = value


def rise(direction, basis, transfers):
    rhs = direction.shape[0]
    depth, rank = transfers.shape[:2]
    return pl.pallas_call(
        rise_kernel,
        out_shape=jax.ShapeDtypeStruct((depth + 1, rhs, rank), jnp.float32),
        compiler_params=pltpu.CompilerParams(vmem_limit_bytes=VMEM_LIMIT),
        cost_estimate=pl.CostEstimate(
            flops=2 * rhs * rank * (basis.shape[1] + 6 * depth * rank),
            bytes_accessed=5 << 20,
            transcendentals=0,
        ),
        name="rise",
    )(direction, basis, transfers)


def near_kernel(crossing, coords, rhs, *refs):
    if crossing:
        (lists, before, first_ref, turned, own, ahead, behind, start, out, acc) = refs
    else:
        (lists, before, first_ref, turned, own, out, acc) = refs
    leaves, partners = lists.shape
    leaf = turned.shape[0] // leaves
    deep = coords + EXTRA
    scale = 2.0 * SHARPNESS * math.log2(math.e)
    first = first_ref[0]
    target = pl.program_id(0)
    mine = pl.multiple_of(target * leaf, leaf)

    def product(ref, slot):
        cols = pl.ds(pl.multiple_of(slot * leaf, leaf), leaf)
        exponent = jnp.dot(
            turned[pl.ds(mine, leaf), 0:deep],
            ref[0:deep, cols],
            preferred_element_type=jnp.float32,
        )
        tile = jnp.exp2(exponent * scale).astype(jnp.bfloat16)
        return lax.dot_general(tile, ref[deep:, cols], NT, preferred_element_type=jnp.float32)

    def lists_me(ref, row):
        found = ref[row, 0] == first + target
        for m in range(1, partners):
            found = found | (ref[row, m] == first + target)
        return found

    if crossing:
        acc[...] = jnp.zeros_like(acc)
    else:
        count = jnp.int32(1)
        for m in range(partners):
            count += jnp.where(lists[target, m] >= 0, 1, 0)
        for a in range(leaves):
            count += jnp.where(lists_me(lists, a), 1, 0)
            count += jnp.where(lists_me(before, a), 1, 0)
        acc[...] = product(own, target) * count.astype(jnp.float32)

    def forward(m, carry):
        slot = lists[target, m] - first
        known = lists[target, m] >= 0
        if crossing:

            @pl.when(known & (slot >= leaves))
            def _():
                acc[...] += product(ahead, slot - leaves)
        else:

            @pl.when(known & (slot < leaves))
            def _():
                acc[...] += product(own, slot)

        return carry

    def backward(a, carry):
        @pl.when(lists_me(before if crossing else lists, a))
        def _():
            acc[...] += product(behind if crossing else own, a)

        return carry

    lax.fori_loop(0, partners, forward, 0)
    if crossing:
        lax.fori_loop(target, leaves, backward, 0)
        out[...] = acc[...].T + start[...]
    else:
        lax.fori_loop(0, target, backward, 0)
        out[...] = acc[...].T


def near_terms(crossing, lists, before, first, turned, own, coords, ahead=None, behind=None, start=None):
    leaves = lists.shape[0]
    height, slab = own.shape
    rhs = height - coords - EXTRA
    leaf = slab // leaves
    smem = pl.BlockSpec(memory_space=pltpu.SMEM)
    vmem = pl.BlockSpec(memory_space=pltpu.VMEM)
    block = pl.BlockSpec((rhs, leaf), lambda j: (0, j))
    args = [lists, before, first, turned, own]
    specs = [smem, smem, smem, vmem, vmem]
    if crossing:
        args += [ahead, behind, start]
        specs += [vmem, vmem, block]
    tiles = 5 * leaves
    return pl.pallas_call(
        functools.partial(near_kernel, crossing, coords, rhs),
        grid=(leaves,),
        in_specs=specs,
        out_specs=block,
        out_shape=jax.ShapeDtypeStruct((rhs, slab), jnp.float32),
        scratch_shapes=[pltpu.VMEM((leaf, rhs), jnp.float32)],
        compiler_params=pltpu.CompilerParams(vmem_limit_bytes=VMEM_LIMIT),
        cost_estimate=pl.CostEstimate(
            flops=tiles * 8 * leaf * leaf * LANES,
            bytes_accessed=4 << 20,
            transcendentals=tiles * leaf * leaf,
        ),
        name="near_crossing" if crossing else "near_own",
    )(*args)


def image_kernel(
    count, totals_ref, transfers_ref, couplings_ref, basis_ref, direction_ref, residual_ref,
    near_ref, image_ref, factors_ref, tall, inner, outer, send_in, recv_in, send_out, recv_out,
):
    me = lax.axis_index("leaf")
    groups = count // GROUP
    base = (me // GROUP) * GROUP
    in_peers = [base + (me - base + d) % GROUP for d in range(1, GROUP)]
    out_peers = [(me + GROUP * e) % count for e in range(1, groups)]
    barrier = pltpu.get_barrier_semaphore()
    for peer in in_peers + out_peers:
        pl.semaphore_signal(barrier, inc=1, device_id=(peer,), device_id_type=MESH)

    depth = transfers_ref.shape[0]
    rhs = direction_ref.shape[0]

    def couple(k):
        halfway = jnp.dot(
            totals_ref[k], couplings_ref[k], precision=HIGHEST, preferred_element_type=jnp.float32
        )
        return lax.dot_general(
            halfway, couplings_ref[k], NT, precision=HIGHEST, preferred_element_type=jnp.float32
        )

    descent = couple(depth)
    for k in reversed(range(depth)):
        descent = lax.dot_general(
            descent, transfers_ref[k], NT, precision=HIGHEST, preferred_element_type=jnp.float32
        ) + couple(k)
    descent = descent.astype(jnp.bfloat16)

    slab = direction_ref.shape[1]
    width = 512

    def block(j, sums):
        cols = pl.ds(pl.multiple_of(j * width, width), width)
        far = jnp.dot(descent, basis_ref[:, cols], preferred_element_type=jnp.float32)
        d = direction_ref[:, cols]
        r = residual_ref[:, cols]
        image = d + near_ref[:, cols] + far
        image_ref[:, cols] = image
        pairs = ((r, r), (d, image), (r, image), (image, image))
        return tuple(
            s + sum((x * y)[:, i : i + LANES] for i in range(0, width, LANES))
            for s, (x, y) in zip(sums, pairs)
        )

    zero = jnp.zeros((rhs, LANES), jnp.float32)
    sums = lax.fori_loop(0, slab // width, block, (zero,) * 4)
    lane = lax.broadcasted_iota(jnp.int32, (rhs, LANES), 1)
    packed = zero
    for i, s in enumerate(sums):
        packed = jnp.where(lane == i, jnp.sum(s, axis=1, keepdims=True), packed)
    tall[...] = jnp.zeros_like(tall)
    tall[0:rhs, :] = packed
    inner[0] = tall[...].T[0:8, :]

    pl.semaphore_wait(barrier, len(in_peers) + len(out_peers))

    def exchange(buffer, peers, send, recv):
        copies = []
        for i, peer in enumerate(peers):
            copy = pltpu.make_async_remote_copy(
                src_ref=buffer.at[0],
                dst_ref=buffer.at[i + 1],
                send_sem=send.at[i],
                recv_sem=recv.at[i],
                device_id=(peer,),
                device_id_type=MESH,
            )
            copy.start()
            copies.append(copy)
        for copy in copies:
            copy.wait()
        total = buffer[0]
        for i in range(len(peers)):
            total = total + buffer[i + 1]
        return total

    total = exchange(inner, in_peers, send_in, recv_in)
    if groups > 1:
        outer[0] = total
        total = exchange(outer, out_peers, send_out, recv_out)
    old = total[0:1]
    step = old / (total[1:2] + EPSILON)
    new = jnp.maximum(old - 2.0 * step * total[2:3] + step * step * total[3:4], 0.0)
    ratio = new / (old + EPSILON)
    row = lax.broadcasted_iota(jnp.int32, (LANES, LANES), 0)
    both = jnp.where(row == 0, step, jnp.where(row == 1, ratio, 0.0))
    factors_ref[...] = both.T[0:rhs, :]


def image_and_factors(totals, transfers, couplings, basis, direction, residual, near):
    count = lax.axis_size("leaf")
    groups = count // GROUP
    rhs, slab = direction.shape
    return pl.pallas_call(
        functools.partial(image_kernel, count),
        out_shape=[
            jax.ShapeDtypeStruct((rhs, slab), jnp.float32),
            jax.ShapeDtypeStruct((rhs, LANES), jnp.float32),
        ],
        scratch_shapes=[
            pltpu.VMEM((LANES, LANES), jnp.float32),
            pltpu.VMEM((GROUP, 8, LANES), jnp.float32),
            pltpu.VMEM((max(groups, 2), 8, LANES), jnp.float32),
            pltpu.SemaphoreType.DMA((GROUP - 1,)),
            pltpu.SemaphoreType.DMA((GROUP - 1,)),
            pltpu.SemaphoreType.DMA((max(groups - 1, 1),)),
            pltpu.SemaphoreType.DMA((max(groups - 1, 1),)),
        ],
        compiler_params=pltpu.CompilerParams(
            vmem_limit_bytes=VMEM_LIMIT, collective_id=0, has_side_effects=True
        ),
        cost_estimate=pl.CostEstimate(
            flops=2 * rhs * slab * basis.shape[0], bytes_accessed=10 << 20, transcendentals=0
        ),
        name="image",
    )(totals, transfers, couplings, basis, direction, residual, near)


def update_kernel(factors, solution, residual, direction, image, new_solution, new_residual, new_direction):
    step = factors[:, 0:1]
    ratio = factors[:, 1:2]
    d = direction[...]
    new_solution[...] = solution[...] + step * d
    r = residual[...] - step * image[...]
    new_residual[...] = r
    new_direction[...] = r + ratio * d


def update(factors, solution, residual, direction, image):
    rhs, slab = direction.shape
    width = slab // 4
    block = pl.BlockSpec((rhs, width), lambda j: (0, j))
    shape = jax.ShapeDtypeStruct((rhs, slab), jnp.float32)
    return pl.pallas_call(
        update_kernel,
        grid=(slab // width,),
        in_specs=[pl.BlockSpec((rhs, LANES), lambda j: (0, 0))] + [block] * 4,
        out_specs=[block] * 3,
        out_shape=[shape] * 3,
        compiler_params=pltpu.CompilerParams(vmem_limit_bytes=VMEM_LIMIT),
        name="update",
    )(factors, solution, residual, direction, image)


def local(
    points, leaf_order, near_pairs, solution, residual, direction, skeleton_basis, transfers, couplings
):
    depth = transfers.shape[0]
    leaves = near_pairs.shape[0]
    coords = points.shape[0]
    leaf = points.shape[1] // leaves
    bits = lax.axis_size("leaf").bit_length() - 1
    first = (lax.axis_index("leaf") * leaves).astype(jnp.int32).reshape(1)
    before = shifted(near_pairs, "leaf", 1, wrap=True)
    running = rise(direction, skeleton_basis, transfers)
    own, turned = arrange(points, leaf_order, direction, leaf)
    ahead = shifted(own, "leaf", -1)
    behind = shifted(own, "leaf", 1)
    totals = []
    for bit in range(bits):
        running = running + swapped(running, "leaf", bit)
        if bit < depth:
            totals.append(running[0])
            running = running[1:]
    totals.append(running[0])
    near = near_terms(False, near_pairs, before, first, turned, own, coords)
    near = near_terms(
        True, near_pairs, before, first, turned, own, coords, ahead, behind, near
    )
    image, factors = image_and_factors(
        jnp.stack(totals), transfers, couplings, skeleton_basis, direction, residual, near
    )
    return tuple(update(factors, solution, residual, direction, image))


def solution(mesh):
    in_specs = (
        P(None, "leaf"),
        P("leaf"),
        P("leaf", None),
        P(None, "leaf"),
        P(None, "leaf"),
        P(None, "leaf"),
        P(None, "leaf"),
        P("leaf", None, None),
        P(),
    )
    out_specs = (P(None, "leaf"), P(None, "leaf"), P(None, "leaf"))
    return jax.shard_map(local, mesh=mesh, in_specs=in_specs, out_specs=out_specs, check_vma=False)
```

```python
import functools

import jax
import jax.numpy as jnp
from jax import lax
from jax.experimental import pallas as pl
from jax.experimental.pallas import tpu as pltpu
from jax.sharding import PartitionSpec as P

SHARPNESS = 2.0
EPSILON = 1e-06
HIGHEST = lax.Precision.HIGHEST
MESH = pl.DeviceIdType.MESH
LANES = 128
EXTRA = 16
GROUP = 8
VMEM_LIMIT = 56 * 1024 * 1024
NT = (((1,), (1,)), ((), ()))


def shifted(x, axis, by):
    peers = lax.axis_size(axis)
    return lax.ppermute(x, axis, [(i, (i + by) % peers) for i in range(peers)])


def f32_dot(a, b):
    return jnp.dot(a, b, precision=HIGHEST, preferred_element_type=jnp.float32)


def f32_dot_nt(a, b):
    return lax.dot_general(a, b, NT, precision=HIGHEST, preferred_element_type=jnp.float32)


def exchange_kernel(
    count, leaf, points_ref, order_ref, direction_ref, basis_ref, transfers_hbm, couplings_hbm,
    window_ref, turned_ref, descent_ref, tall, transfers, couplings, skel, cur, arrived, coupled,
    load_sem, own_send, own_recv, stage_send, stage_recv, swap_send, swap_recv,
):
    coords, slab = points_ref.shape
    rhs = direction_ref.shape[0]
    depth = transfers.shape[0]
    bits = count.bit_length() - 1
    leaves = slab // leaf
    chunks = slab // LANES
    half = rhs // 2
    me = lax.axis_index("leaf")
    load_t = pltpu.make_async_copy(transfers_hbm, transfers, load_sem.at[0])
    load_c = pltpu.make_async_copy(couplings_hbm, couplings, load_sem.at[1])
    load_t.start()
    load_c.start()
    after, prior = (me + 1) % count, (me + count - 1) % count
    peers = [me + (1 << b) * (1 - 2 * ((me // (1 << b)) % 2)) for b in range(bits)]
    barrier = pltpu.get_barrier_semaphore()
    for peer in [after, prior] + peers:
        pl.semaphore_signal(barrier, inc=1, device_id=(peer,), device_id_type=MESH)

    value = lax.dot_general(
        direction_ref[...].astype(jnp.bfloat16),
        basis_ref[...],
        NT,
        preferred_element_type=jnp.float32,
    )
    skel[0] = value
    load_t.wait()
    for k in range(depth):
        value = f32_dot(value, transfers[k])
        skel[k + 1] = value
    pl.semaphore_wait(barrier, 2 + bits)

    mine = pl.multiple_of((me % 2) * half, half)
    other = pl.multiple_of((1 - me % 2) * half, half)

    def stage(b):
        low = min(b, depth)
        return pltpu.make_async_remote_copy(
            src_ref=skel.at[:, pl.ds(other, half)] if b == 0 else cur.at[pl.ds(low, depth + 1 - low)],
            dst_ref=arrived.at[b, pl.ds(low, depth + 1 - low)],
            send_sem=stage_send.at[b],
            recv_sem=stage_recv.at[b],
            device_id=(peers[b],),
            device_id_type=MESH,
        )

    def place(j, slot):
        return pl.ds(pl.multiple_of(slot * slab + j * leaf, leaf), leaf)

    def to_prior(j):
        return pltpu.make_async_remote_copy(
            src_ref=window_ref.at[:, place(j, 1)],
            dst_ref=window_ref.at[:, place(j, 2)],
            send_sem=own_send.at[0, j],
            recv_sem=own_recv.at[0, j],
            device_id=(prior,),
            device_id_type=MESH,
        )

    def to_after(j):
        return pltpu.make_async_remote_copy(
            src_ref=window_ref.at[:, place(j, 1)],
            dst_ref=window_ref.at[:, place(j, 0)],
            send_sem=own_send.at[1, j],
            recv_sem=own_recv.at[1, j],
            device_id=(after,),
            device_id_type=MESH,
        )

    def arrange(j, carry):
        cols = pl.ds(pl.multiple_of(j * leaf, leaf), leaf)
        order = order_ref[:, cols]
        high = order // LANES
        low = order - high * LANES
        rows = lax.broadcasted_iota(jnp.int32, (LANES, leaf), 0)
        onehot = jnp.where(rows == low, 1.0, 0.0).astype(jnp.bfloat16)
        picked = jnp.zeros((coords, leaf), jnp.float32)
        step = 4
        for c in range(0, chunks, step):
            part = jnp.dot(
                tall[c * coords : (c + step) * coords, :], onehot, preferred_element_type=jnp.float32
            )
            for h in range(step):
                picked = jnp.where(high == c + h, part[h * coords : (h + 1) * coords], picked)
        square = -0.5 * jnp.sum(picked * picked, axis=0, keepdims=True)
        first = square.astype(jnp.bfloat16).astype(jnp.float32)
        second = (square - first).astype(jnp.bfloat16).astype(jnp.float32)
        third = (square - first - second).astype(jnp.bfloat16).astype(jnp.float32)

        def extra(height, at_parts, at_ones):
            row = lax.broadcasted_iota(jnp.int32, (height, leaf), 0)
            out = jnp.where((row >= at_ones) & (row < at_ones + 3), 1.0, 0.0)
            for i, piece in enumerate((first, second, third)):
                out = jnp.where(row == at_parts + i, piece, out)
            return out

        here = place(j, 1)
        window_ref[0:coords, here] = picked.astype(jnp.bfloat16)
        window_ref[coords : coords + EXTRA, here] = extra(EXTRA, 0, 3).astype(jnp.bfloat16)
        window_ref[coords + EXTRA :, here] = direction_ref[:, cols].astype(jnp.bfloat16)

        @pl.when(me > 0)
        def _():
            to_prior(j).start()

        @pl.when(me < count - 1)
        def _():
            to_after(j).start()

        wide = jnp.concatenate([picked, extra(LANES - coords, 3, 0)], axis=0)
        turned_ref[cols, :] = (2.0 * SHARPNESS * wide.T).astype(jnp.bfloat16)
        return carry

    def swap(k):
        return pltpu.make_async_remote_copy(
            src_ref=coupled.at[k, me % 2],
            dst_ref=coupled.at[k, me % 2],
            send_sem=swap_send.at[k],
            recv_sem=swap_recv.at[k],
            device_id=(peers[0],),
            device_id_type=MESH,
        )

    def couple(k):
        coupled[k, me % 2] = f32_dot_nt(f32_dot(cur[k], couplings[k]), couplings[k])
        swap(k).start()

    def both_halves(k):
        swap(k).wait()
        return coupled[k].reshape(rhs, coupled.shape[-1])

    stage(0).start()
    for h in range(chunks):
        tall[h * coords : (h + 1) * coords, :] = points_ref[:, h * LANES : (h + 1) * LANES]
    done = 0
    for b in range(bits):
        upto = min(leaves, -(-leaves * (b + 1) // min(bits, depth)))
        if upto > done:
            lax.fori_loop(done, upto, arrange, 0)
        done = upto
        stage(b).wait()
        low = min(b, depth)
        if b == 0:
            cur[...] = skel[:, pl.ds(mine, half)] + arrived[0]
        else:
            cur[low:] = cur[low:] + arrived[b, low:]
        if b + 1 < bits:
            stage(b + 1).start()
        if b == 0:
            load_c.wait()
        if b < depth:
            couple(b)
    couple(depth)
    descent = both_halves(depth)
    for k in reversed(range(depth)):
        descent = f32_dot_nt(descent, transfers[k]) + both_halves(k)
    descent_ref[...] = descent.astype(jnp.bfloat16)

    def finish(j, carry):
        @pl.when(me > 0)
        def _():
            to_prior(j).wait_send()
            to_after(j).wait_recv()

        @pl.when(me < count - 1)
        def _():
            to_after(j).wait_send()
            to_prior(j).wait_recv()

        return carry

    lax.fori_loop(0, leaves, finish, 0)


def exchange(points, leaf_order, direction, basis, transfers, couplings, leaf):
    count = lax.axis_size("leaf")
    bits = count.bit_length() - 1
    coords, slab = points.shape
    rhs = direction.shape[0]
    depth, rank = transfers.shape[:2]
    leaves = slab // leaf
    height = coords + EXTRA + rhs
    vmem = pl.BlockSpec(memory_space=pltpu.VMEM)
    hbm = pl.BlockSpec(memory_space=pl.ANY)
    half = (depth + 1, rhs // 2, rank)
    return pl.pallas_call(
        functools.partial(exchange_kernel, count, leaf),
        in_specs=[vmem] * 4 + [hbm] * 2,
        out_specs=[vmem] * 3,
        out_shape=[
            jax.ShapeDtypeStruct((height, 3 * slab), jnp.bfloat16),
            jax.ShapeDtypeStruct((slab, LANES), jnp.bfloat16),
            jax.ShapeDtypeStruct((rhs, rank), jnp.bfloat16),
        ],
        scratch_shapes=[
            pltpu.VMEM((slab // LANES * coords, LANES), jnp.bfloat16),
            pltpu.VMEM(transfers.shape, jnp.float32),
            pltpu.VMEM(couplings.shape, jnp.float32),
            pltpu.VMEM((depth + 1, rhs, rank), jnp.float32),
            pltpu.VMEM(half, jnp.float32),
            pltpu.VMEM((bits,) + half, jnp.float32),
            pltpu.VMEM((depth + 1, 2, rhs // 2, rank), jnp.float32),
            pltpu.SemaphoreType.DMA((2,)),
            pltpu.SemaphoreType.DMA((2, leaves)),
            pltpu.SemaphoreType.DMA((2, leaves)),
            pltpu.SemaphoreType.DMA((bits,)),
            pltpu.SemaphoreType.DMA((bits,)),
            pltpu.SemaphoreType.DMA((depth + 1,)),
            pltpu.SemaphoreType.DMA((depth + 1,)),
        ],
        compiler_params=pltpu.CompilerParams(
            vmem_limit_bytes=VMEM_LIMIT, collective_id=1, has_side_effects=True
        ),
        cost_estimate=pl.CostEstimate(
            flops=2 * coords * slab * slab, bytes_accessed=10 << 20, transcendentals=0
        ),
        name="exchange",
    )(points, leaf_order.reshape(1, slab), direction, basis, transfers, couplings)


def near_kernel(
    coords, lists, before, first_ref, turned, window, descent, basis, direction, residual,
    image_ref, sums_ref, acc, slots,
):
    leaves, partners = lists.shape
    leaf = turned.shape[0]
    rhs = direction.shape[0]
    deep = coords + EXTRA
    target = pl.program_id(0)
    whole_id = first_ref[0] + target

    def lists_me(ref, row):
        found = ref[row, 0] == whole_id
        for m in range(1, partners):
            found = found | (ref[row, m] == whole_id)
        return found

    known = jnp.int32(0)
    for m in range(partners):
        slots[known] = lists[target, m] - first_ref[0] + leaves
        known += jnp.where(lists[target, m] >= 0, 1, 0)
    for ref, at in ((lists, leaves), (before, 0)):
        for a in range(leaves):
            slots[known] = a + at
            known += jnp.where(lists_me(ref, a), 1, 0)
    slots[known] = target + leaves
    slots[known + 1] = target + leaves
    acc[...] = jnp.zeros_like(acc)
    rows = 128

    def two(i, carry):
        cols, weights = [], []
        for s in range(2):
            at = 2 * i + s
            cols.append(pl.ds(pl.multiple_of(slots[at] * leaf, leaf), leaf))
            weight = jnp.where(at < known, 1, jnp.where(at == known, 1 + known, 0))
            weights.append(weight.astype(jnp.float32))
        for r in range(0, leaf, rows):
            total = acc[r : r + rows, :]
            for col, weight in zip(cols, weights):
                exponent = jnp.dot(
                    turned[r : r + rows, 0:deep],
                    window[0:deep, col],
                    preferred_element_type=jnp.float32,
                )
                tile = jnp.exp(exponent).astype(jnp.bfloat16)
                total += weight * lax.dot_general(
                    tile, window[deep:, col], NT, preferred_element_type=jnp.float32
                )
            acc[r : r + rows, :] = total
        return carry

    lax.fori_loop(0, (known + 2) // 2, two, 0)
    d = direction[...]
    r = residual[...]
    image = d + acc[...].T + jnp.dot(descent[...], basis[...], preferred_element_type=jnp.float32)
    image_ref[...] = image

    @pl.when(target == 0)
    def _():
        sums_ref[...] = jnp.zeros_like(sums_ref)

    for q, (x, y) in enumerate(((r, r), (d, image), (r, image), (image, image))):
        both = x * y
        sums_ref[q] += sum(both[:, i : i + LANES] for i in range(0, leaf, LANES))


def near_and_image(lists, before, first, turned, window, descent, basis, direction, residual, coords):
    leaves, partners = lists.shape
    rhs, slab = direction.shape
    rank = basis.shape[0]
    leaf = slab // leaves
    smem = pl.BlockSpec(memory_space=pltpu.SMEM)
    vmem = pl.BlockSpec(memory_space=pltpu.VMEM)
    block = pl.BlockSpec((rhs, leaf), lambda j: (0, j))
    return pl.pallas_call(
        functools.partial(near_kernel, coords),
        grid=(leaves,),
        in_specs=[
            smem, smem, smem,
            pl.BlockSpec((leaf, LANES), lambda j: (j, 0)),
            vmem, vmem,
            pl.BlockSpec((rank, leaf), lambda j: (0, j)),
            block, block,
        ],
        out_specs=[block, pl.BlockSpec((4, rhs, LANES), lambda j: (0, 0, 0))],
        out_shape=[
            jax.ShapeDtypeStruct((rhs, slab), jnp.float32),
            jax.ShapeDtypeStruct((4, rhs, LANES), jnp.float32),
        ],
        scratch_shapes=[
            pltpu.VMEM((leaf, rhs), jnp.float32),
            pltpu.SMEM((partners + 2 * leaves + 2,), jnp.int32),
        ],
        compiler_params=pltpu.CompilerParams(vmem_limit_bytes=VMEM_LIMIT),
        name="near",
    )(lists, before, first, turned, window, descent, basis, direction, residual)


def reduce_kernel(
    count, sums_ref, factors_ref, tall, inner, outer, send_in, recv_in, send_out, recv_out
):
    me = lax.axis_index("leaf")
    groups = count // GROUP
    base = (me // GROUP) * GROUP
    in_peers = [base + (me - base + d) % GROUP for d in range(1, GROUP)]
    out_peers = [(me + GROUP * e) % count for e in range(1, groups)]
    barrier = pltpu.get_barrier_semaphore()
    for peer in in_peers + out_peers:
        pl.semaphore_signal(barrier, inc=1, device_id=(peer,), device_id_type=MESH)

    rhs = sums_ref.shape[1]
    sums = [sums_ref[q] for q in range(4)]
    zero = jnp.zeros((rhs, LANES), jnp.float32)
    lane = lax.broadcasted_iota(jnp.int32, (rhs, LANES), 1)
    packed = zero
    for i, s in enumerate(sums):
        packed = jnp.where(lane == i, jnp.sum(s, axis=1, keepdims=True), packed)
    tall[...] = jnp.zeros_like(tall)
    tall[0:rhs, :] = packed
    inner[0] = tall[...].T[0:8, :]

    pl.semaphore_wait(barrier, len(in_peers) + len(out_peers))

    def all_sum(buffer, peers, send, recv):
        copies = []
        for i, peer in enumerate(peers):
            copy = pltpu.make_async_remote_copy(
                src_ref=buffer.at[0],
                dst_ref=buffer.at[i + 1],
                send_sem=send.at[i],
                recv_sem=recv.at[i],
                device_id=(peer,),
                device_id_type=MESH,
            )
            copy.start()
            copies.append(copy)
        for copy in copies:
            copy.wait()
        total = buffer[0]
        for i in range(len(peers)):
            total = total + buffer[i + 1]
        return total

    total = all_sum(inner, in_peers, send_in, recv_in)
    if groups > 1:
        outer[0] = total
        total = all_sum(outer, out_peers, send_out, recv_out)
    old = total[0:1]
    step = old / (total[1:2] + EPSILON)
    new = jnp.maximum(old - 2.0 * step * total[2:3] + step * step * total[3:4], 0.0)
    ratio = new / (old + EPSILON)
    row = lax.broadcasted_iota(jnp.int32, (LANES, LANES), 0)
    both = jnp.where(row == 0, step, jnp.where(row == 1, ratio, 0.0))
    factors_ref[...] = both.T[0:rhs, :]


def reduce(sums):
    count = lax.axis_size("leaf")
    groups = count // GROUP
    rhs = sums.shape[1]
    vmem = pl.BlockSpec(memory_space=pltpu.VMEM)
    return pl.pallas_call(
        functools.partial(reduce_kernel, count),
        in_specs=[vmem],
        out_specs=vmem,
        out_shape=jax.ShapeDtypeStruct((rhs, LANES), jnp.float32),
        scratch_shapes=[
            pltpu.VMEM((LANES, LANES), jnp.float32),
            pltpu.VMEM((GROUP, 8, LANES), jnp.float32),
            pltpu.VMEM((max(groups, 2), 8, LANES), jnp.float32),
            pltpu.SemaphoreType.DMA((GROUP - 1,)),
            pltpu.SemaphoreType.DMA((GROUP - 1,)),
            pltpu.SemaphoreType.DMA((max(groups - 1, 1),)),
            pltpu.SemaphoreType.DMA((max(groups - 1, 1),)),
        ],
        compiler_params=pltpu.CompilerParams(
            vmem_limit_bytes=VMEM_LIMIT, collective_id=0, has_side_effects=True
        ),
        name="reduce",
    )(sums)


def update_kernel(factors, solution, residual, direction, image, new_solution, new_residual, new_direction):
    step = factors[:, 0:1]
    ratio = factors[:, 1:2]
    d = direction[...]
    new_solution[...] = solution[...] + step * d
    r = residual[...] - step * image[...]
    new_residual[...] = r
    new_direction[...] = r + ratio * d


def update(factors, solution, residual, direction, image):
    rhs, slab = direction.shape
    width = slab // 4
    block = pl.BlockSpec((rhs, width), lambda j: (0, j))
    shape = jax.ShapeDtypeStruct((rhs, slab), jnp.float32)
    return pl.pallas_call(
        update_kernel,
        grid=(slab // width,),
        in_specs=[pl.BlockSpec((rhs, LANES), lambda j: (0, 0))] + [block] * 4,
        out_specs=[block] * 3,
        out_shape=[shape] * 3,
        compiler_params=pltpu.CompilerParams(vmem_limit_bytes=VMEM_LIMIT),
        name="update",
    )(factors, solution, residual, direction, image)


def local(
    points, leaf_order, near_pairs, solution, residual, direction, skeleton_basis, transfers, couplings
):
    leaves = near_pairs.shape[0]
    leaf = points.shape[1] // leaves
    first = (lax.axis_index("leaf") * leaves).astype(jnp.int32).reshape(1)
    before = shifted(near_pairs, "leaf", 1)
    window, turned, descent = exchange(
        points, leaf_order, direction, skeleton_basis, transfers, couplings, leaf
    )
    image, sums = near_and_image(
        near_pairs, before, first, turned, window, descent, skeleton_basis, direction, residual,
        points.shape[0],
    )
    factors = reduce(sums)
    return tuple(update(factors, solution, residual, direction, image))


def solution(mesh):
    in_specs = (
        P(None, "leaf"),
        P("leaf"),
        P("leaf", None),
        P(None, "leaf"),
        P(None, "leaf"),
        P(None, "leaf"),
        P(None, "leaf"),
        P("leaf", None, None),
        P(),
    )
    out_specs = (P(None, "leaf"), P(None, "leaf"), P(None, "leaf"))
    return jax.shard_map(local, mesh=mesh, in_specs=in_specs, out_specs=out_specs, check_vma=False)
```

```python
import functools

import jax
import jax.numpy as jnp
from jax import lax
from jax.experimental import pallas as pl
from jax.experimental.pallas import tpu as pltpu
from jax.sharding import PartitionSpec as P

SHARPNESS = 2.0
EPSILON = 1e-06
HIGHEST = lax.Precision.HIGHEST
MESH = pl.DeviceIdType.MESH
LANES = 128
EXTRA = 16
GROUP = 8
VMEM_LIMIT = 56 * 1024 * 1024
NT = (((1,), (1,)), ((), ()))


def shifted(x, axis, by):
    peers = lax.axis_size(axis)
    return lax.ppermute(x, axis, [(i, (i + by) % peers) for i in range(peers)])


def f32_dot(a, b):
    return jnp.dot(a, b, precision=HIGHEST, preferred_element_type=jnp.float32)


def f32_dot_nt(a, b):
    return lax.dot_general(a, b, NT, precision=HIGHEST, preferred_element_type=jnp.float32)


def exchange_kernel(
    count, leaf, points_ref, order_ref, direction_ref, basis_ref, transfers_hbm, couplings_hbm,
    window_ref, turned_ref, descent_ref, tall, transfers, couplings, skel, cur, arrived, coupled,
    load_sem, own_send, own_recv, stage_send, stage_recv, swap_send, swap_recv,
):
    coords, slab = points_ref.shape
    rhs = direction_ref.shape[0]
    depth = transfers.shape[0]
    bits = count.bit_length() - 1
    leaves = slab // leaf
    chunks = slab // LANES
    half = rhs // 2
    me = lax.axis_index("leaf")
    load_t = pltpu.make_async_copy(transfers_hbm, transfers, load_sem.at[0])
    load_c = pltpu.make_async_copy(couplings_hbm, couplings, load_sem.at[1])
    load_t.start()
    load_c.start()
    after, prior = (me + 1) % count, (me + count - 1) % count
    peers = [me + (1 << b) * (1 - 2 * ((me // (1 << b)) % 2)) for b in range(bits)]
    barrier = pltpu.get_barrier_semaphore()
    for peer in [after, prior] + peers:
        pl.semaphore_signal(barrier, inc=1, device_id=(peer,), device_id_type=MESH)

    for h in range(chunks):
        tall[h * coords : (h + 1) * coords, :] = points_ref[:, h * LANES : (h + 1) * LANES]
    pl.semaphore_wait(barrier, 2 + bits)

    mine = pl.multiple_of((me % 2) * half, half)
    other = pl.multiple_of((1 - me % 2) * half, half)

    def stage(b):
        low = min(b, depth)
        return pltpu.make_async_remote_copy(
            src_ref=skel.at[:, pl.ds(other, half)] if b == 0 else cur.at[pl.ds(low, depth + 1 - low)],
            dst_ref=arrived.at[b, pl.ds(low, depth + 1 - low)],
            send_sem=stage_send.at[b],
            recv_sem=stage_recv.at[b],
            device_id=(peers[b],),
            device_id_type=MESH,
        )

    def place(j, slot):
        return pl.ds(pl.multiple_of(slot * slab + j * leaf, leaf), leaf)

    def to_prior(j):
        return pltpu.make_async_remote_copy(
            src_ref=window_ref.at[:, place(j, 1)],
            dst_ref=window_ref.at[:, place(j, 2)],
            send_sem=own_send.at[0, j],
            recv_sem=own_recv.at[0, j],
            device_id=(prior,),
            device_id_type=MESH,
        )

    def to_after(j):
        return pltpu.make_async_remote_copy(
            src_ref=window_ref.at[:, place(j, 1)],
            dst_ref=window_ref.at[:, place(j, 0)],
            send_sem=own_send.at[1, j],
            recv_sem=own_recv.at[1, j],
            device_id=(after,),
            device_id_type=MESH,
        )

    def arrange(j, carry):
        cols = pl.ds(pl.multiple_of(j * leaf, leaf), leaf)
        order = order_ref[:, cols]
        high = order // LANES
        low = order - high * LANES
        rows = lax.broadcasted_iota(jnp.int32, (LANES, leaf), 0)
        onehot = jnp.where(rows == low, 1.0, 0.0).astype(jnp.bfloat16)
        picked = jnp.zeros((coords, leaf), jnp.float32)
        step = 4
        for c in range(0, chunks, step):
            part = jnp.dot(
                tall[c * coords : (c + step) * coords, :], onehot, preferred_element_type=jnp.float32
            )
            for h in range(step):
                picked = jnp.where(high == c + h, part[h * coords : (h + 1) * coords], picked)
        square = -0.5 * jnp.sum(picked * picked, axis=0, keepdims=True)
        first = square.astype(jnp.bfloat16).astype(jnp.float32)
        second = (square - first).astype(jnp.bfloat16).astype(jnp.float32)
        third = (square - first - second).astype(jnp.bfloat16).astype(jnp.float32)

        def extra(height, at_parts, at_ones):
            row = lax.broadcasted_iota(jnp.int32, (height, leaf), 0)
            out = jnp.where((row >= at_ones) & (row < at_ones + 3), 1.0, 0.0)
            for i, piece in enumerate((first, second, third)):
                out = jnp.where(row == at_parts + i, piece, out)
            return out

        here = place(j, 1)
        window_ref[0:coords, here] = picked.astype(jnp.bfloat16)
        window_ref[coords : coords + EXTRA, here] = extra(EXTRA, 0, 3).astype(jnp.bfloat16)
        window_ref[coords + EXTRA :, here] = direction_ref[:, cols].astype(jnp.bfloat16)

        @pl.when(me > 0)
        def _():
            to_prior(j).start()

        @pl.when(me < count - 1)
        def _():
            to_after(j).start()

        wide = jnp.concatenate([picked, extra(LANES - coords, 3, 0)], axis=0)
        turned_ref[cols, :] = (2.0 * SHARPNESS * wide.T).astype(jnp.bfloat16)
        return carry

    def swap(k):
        return pltpu.make_async_remote_copy(
            src_ref=coupled.at[k, me % 2],
            dst_ref=coupled.at[k, me % 2],
            send_sem=swap_send.at[k],
            recv_sem=swap_recv.at[k],
            device_id=(peers[0],),
            device_id_type=MESH,
        )

    def couple(k):
        coupled[k, me % 2] = f32_dot_nt(f32_dot(cur[k], couplings[k]), couplings[k])
        swap(k).start()

    def both_halves(k):
        swap(k).wait()
        return coupled[k].reshape(rhs, coupled.shape[-1])

    done = (leaves + 1) // 2
    lax.fori_loop(0, done, arrange, 0)
    value = lax.dot_general(
        direction_ref[...].astype(jnp.bfloat16),
        basis_ref[...],
        NT,
        preferred_element_type=jnp.float32,
    )
    skel[0] = value
    load_t.wait()
    for k in range(depth):
        value = f32_dot(value, transfers[k])
        skel[k + 1] = value
    stage(0).start()
    for b in range(bits):
        upto = leaves if b + 1 == min(bits, depth) else min(leaves, done + 1)
        if upto > done:
            lax.fori_loop(done, upto, arrange, 0)
        done = upto
        stage(b).wait()
        low = min(b, depth)
        if b == 0:
            cur[...] = skel[:, pl.ds(mine, half)] + arrived[0]
        else:
            cur[low:] = cur[low:] + arrived[b, low:]
        if b + 1 < bits:
            stage(b + 1).start()
        if b == 0:
            load_c.wait()
        if b < depth:
            couple(b)
    couple(depth)
    descent = both_halves(depth)
    for k in reversed(range(depth)):
        descent = f32_dot_nt(descent, transfers[k]) + both_halves(k)
    descent_ref[...] = descent.astype(jnp.bfloat16)

    def finish(j, carry):
        @pl.when(me > 0)
        def _():
            to_prior(j).wait_send()
            to_after(j).wait_recv()

        @pl.when(me < count - 1)
        def _():
            to_after(j).wait_send()
            to_prior(j).wait_recv()

        return carry

    lax.fori_loop(0, leaves, finish, 0)


def exchange(points, leaf_order, direction, basis, transfers, couplings, leaf):
    count = lax.axis_size("leaf")
    bits = count.bit_length() - 1
    coords, slab = points.shape
    rhs = direction.shape[0]
    depth, rank = transfers.shape[:2]
    leaves = slab // leaf
    height = coords + EXTRA + rhs
    vmem = pl.BlockSpec(memory_space=pltpu.VMEM)
    hbm = pl.BlockSpec(memory_space=pl.ANY)
    half = (depth + 1, rhs // 2, rank)
    return pl.pallas_call(
        functools.partial(exchange_kernel, count, leaf),
        in_specs=[vmem] * 4 + [hbm] * 2,
        out_specs=[vmem] * 3,
        out_shape=[
            jax.ShapeDtypeStruct((height, 3 * slab), jnp.bfloat16),
            jax.ShapeDtypeStruct((slab, LANES), jnp.bfloat16),
            jax.ShapeDtypeStruct((rhs, rank), jnp.bfloat16),
        ],
        scratch_shapes=[
            pltpu.VMEM((slab // LANES * coords, LANES), jnp.bfloat16),
            pltpu.VMEM(transfers.shape, jnp.float32),
            pltpu.VMEM(couplings.shape, jnp.float32),
            pltpu.VMEM((depth + 1, rhs, rank), jnp.float32),
            pltpu.VMEM(half, jnp.float32),
            pltpu.VMEM((bits,) + half, jnp.float32),
            pltpu.VMEM((depth + 1, 2, rhs // 2, rank), jnp.float32),
            pltpu.SemaphoreType.DMA((2,)),
            pltpu.SemaphoreType.DMA((2, leaves)),
            pltpu.SemaphoreType.DMA((2, leaves)),
            pltpu.SemaphoreType.DMA((bits,)),
            pltpu.SemaphoreType.DMA((bits,)),
            pltpu.SemaphoreType.DMA((depth + 1,)),
            pltpu.SemaphoreType.DMA((depth + 1,)),
        ],
        compiler_params=pltpu.CompilerParams(
            vmem_limit_bytes=VMEM_LIMIT, collective_id=1, has_side_effects=True
        ),
        cost_estimate=pl.CostEstimate(
            flops=2 * coords * slab * slab, bytes_accessed=10 << 20, transcendentals=0
        ),
        name="exchange",
    )(points, leaf_order.reshape(1, slab), direction, basis, transfers, couplings)


def near_kernel(
    coords, lists, before, first_ref, turned, window, descent, basis, direction, residual,
    image_ref, sums_ref, acc, slots,
):
    leaves, partners = lists.shape
    leaf = turned.shape[0]
    rhs = direction.shape[0]
    deep = coords + EXTRA
    target = pl.program_id(0)
    whole_id = first_ref[0] + target

    def lists_me(ref, row):
        found = ref[row, 0] == whole_id
        for m in range(1, partners):
            found = found | (ref[row, m] == whole_id)
        return found

    known = jnp.int32(0)
    for m in range(partners):
        slots[known] = lists[target, m] - first_ref[0] + leaves
        known += jnp.where(lists[target, m] >= 0, 1, 0)
    for ref, at in ((lists, leaves), (before, 0)):
        for a in range(leaves):
            slots[known] = a + at
            known += jnp.where(lists_me(ref, a), 1, 0)
    slots[known] = target + leaves
    slots[known + 1] = target + leaves
    acc[...] = jnp.zeros_like(acc)
    rows = leaf

    def two(i, carry):
        cols, weights = [], []
        for s in range(2):
            at = 2 * i + s
            cols.append(pl.ds(pl.multiple_of(slots[at] * leaf, leaf), leaf))
            weight = jnp.where(at < known, 1, jnp.where(at == known, 1 + known, 0))
            weights.append(weight.astype(jnp.float32))
        for r in range(0, leaf, rows):
            total = acc[r : r + rows, :]
            for col, weight in zip(cols, weights):
                exponent = jnp.dot(
                    turned[r : r + rows, 0:deep],
                    window[0:deep, col],
                    preferred_element_type=jnp.float32,
                )
                tile = jnp.exp(exponent).astype(jnp.bfloat16)
                total += weight * lax.dot_general(
                    tile, window[deep:, col], NT, preferred_element_type=jnp.float32
                )
            acc[r : r + rows, :] = total
        return carry

    lax.fori_loop(0, (known + 2) // 2, two, 0)
    d = direction[...]
    r = residual[...]
    image = d + acc[...].T + jnp.dot(descent[...], basis[...], preferred_element_type=jnp.float32)
    image_ref[...] = image

    @pl.when(target == 0)
    def _():
        sums_ref[...] = jnp.zeros_like(sums_ref)

    for q, (x, y) in enumerate(((r, r), (d, image), (r, image), (image, image))):
        both = x * y
        sums_ref[q] += sum(both[:, i : i + LANES] for i in range(0, leaf, LANES))


def near_and_image(lists, before, first, turned, window, descent, basis, direction, residual, coords):
    leaves, partners = lists.shape
    rhs, slab = direction.shape
    rank = basis.shape[0]
    leaf = slab // leaves
    smem = pl.BlockSpec(memory_space=pltpu.SMEM)
    vmem = pl.BlockSpec(memory_space=pltpu.VMEM)
    block = pl.BlockSpec((rhs, leaf), lambda j: (0, j))
    return pl.pallas_call(
        functools.partial(near_kernel, coords),
        grid=(leaves,),
        in_specs=[
            smem, smem, smem,
            pl.BlockSpec((leaf, LANES), lambda j: (j, 0)),
            vmem, vmem,
            pl.BlockSpec((rank, leaf), lambda j: (0, j)),
            block, block,
        ],
        out_specs=[block, pl.BlockSpec((4, rhs, LANES), lambda j: (0, 0, 0))],
        out_shape=[
            jax.ShapeDtypeStruct((rhs, slab), jnp.float32),
            jax.ShapeDtypeStruct((4, rhs, LANES), jnp.float32),
        ],
        scratch_shapes=[
            pltpu.VMEM((leaf, rhs), jnp.float32),
            pltpu.SMEM((partners + 2 * leaves + 2,), jnp.int32),
        ],
        compiler_params=pltpu.CompilerParams(vmem_limit_bytes=VMEM_LIMIT),
        name="near",
    )(lists, before, first, turned, window, descent, basis, direction, residual)


def reduce_kernel(
    count, sums_ref, factors_ref, tall, inner, outer, send_in, recv_in, send_out, recv_out
):
    me = lax.axis_index("leaf")
    groups = count // GROUP
    base = (me // GROUP) * GROUP
    in_peers = [base + (me - base + d) % GROUP for d in range(1, GROUP)]
    out_peers = [(me + GROUP * e) % count for e in range(1, groups)]
    barrier = pltpu.get_barrier_semaphore()
    for peer in in_peers + out_peers:
        pl.semaphore_signal(barrier, inc=1, device_id=(peer,), device_id_type=MESH)

    rhs = sums_ref.shape[1]
    sums = [sums_ref[q] for q in range(4)]
    zero = jnp.zeros((rhs, LANES), jnp.float32)
    lane = lax.broadcasted_iota(jnp.int32, (rhs, LANES), 1)
    packed = zero
    for i, s in enumerate(sums):
        packed = jnp.where(lane == i, jnp.sum(s, axis=1, keepdims=True), packed)
    tall[...] = jnp.zeros_like(tall)
    tall[0:rhs, :] = packed
    inner[0] = tall[...].T[0:8, :]

    pl.semaphore_wait(barrier, len(in_peers) + len(out_peers))

    def all_sum(buffer, peers, send, recv):
        copies = []
        for i, peer in enumerate(peers):
            copy = pltpu.make_async_remote_copy(
                src_ref=buffer.at[0],
                dst_ref=buffer.at[i + 1],
                send_sem=send.at[i],
                recv_sem=recv.at[i],
                device_id=(peer,),
                device_id_type=MESH,
            )
            copy.start()
            copies.append(copy)
        for copy in copies:
            copy.wait()
        total = buffer[0]
        for i in range(len(peers)):
            total = total + buffer[i + 1]
        return total

    total = all_sum(inner, in_peers, send_in, recv_in)
    if groups > 1:
        outer[0] = total
        total = all_sum(outer, out_peers, send_out, recv_out)
    old = total[0:1]
    step = old / (total[1:2] + EPSILON)
    new = jnp.maximum(old - 2.0 * step * total[2:3] + step * step * total[3:4], 0.0)
    ratio = new / (old + EPSILON)
    row = lax.broadcasted_iota(jnp.int32, (LANES, LANES), 0)
    both = jnp.where(row == 0, step, jnp.where(row == 1, ratio, 0.0))
    factors_ref[...] = both.T[0:rhs, :]


def reduce(sums):
    count = lax.axis_size("leaf")
    groups = count // GROUP
    rhs = sums.shape[1]
    vmem = pl.BlockSpec(memory_space=pltpu.VMEM)
    return pl.pallas_call(
        functools.partial(reduce_kernel, count),
        in_specs=[vmem],
        out_specs=vmem,
        out_shape=jax.ShapeDtypeStruct((rhs, LANES), jnp.float32),
        scratch_shapes=[
            pltpu.VMEM((LANES, LANES), jnp.float32),
            pltpu.VMEM((GROUP, 8, LANES), jnp.float32),
            pltpu.VMEM((max(groups, 2), 8, LANES), jnp.float32),
            pltpu.SemaphoreType.DMA((GROUP - 1,)),
            pltpu.SemaphoreType.DMA((GROUP - 1,)),
            pltpu.SemaphoreType.DMA((max(groups - 1, 1),)),
            pltpu.SemaphoreType.DMA((max(groups - 1, 1),)),
        ],
        compiler_params=pltpu.CompilerParams(
            vmem_limit_bytes=VMEM_LIMIT, collective_id=0, has_side_effects=True
        ),
        name="reduce",
    )(sums)


def update_kernel(factors, solution, residual, direction, image, new_solution, new_residual, new_direction):
    step = factors[:, 0:1]
    ratio = factors[:, 1:2]
    d = direction[...]
    new_solution[...] = solution[...] + step * d
    r = residual[...] - step * image[...]
    new_residual[...] = r
    new_direction[...] = r + ratio * d


def update(factors, solution, residual, direction, image):
    rhs, slab = direction.shape
    width = slab // 8
    block = pl.BlockSpec((rhs, width), lambda j: (0, j))
    shape = jax.ShapeDtypeStruct((rhs, slab), jnp.float32)
    return pl.pallas_call(
        update_kernel,
        grid=(slab // width,),
        in_specs=[pl.BlockSpec((rhs, LANES), lambda j: (0, 0))] + [block] * 4,
        out_specs=[block] * 3,
        out_shape=[shape] * 3,
        compiler_params=pltpu.CompilerParams(vmem_limit_bytes=VMEM_LIMIT),
        name="update",
    )(factors, solution, residual, direction, image)


def local(
    points, leaf_order, near_pairs, solution, residual, direction, skeleton_basis, transfers, couplings
):
    leaves = near_pairs.shape[0]
    leaf = points.shape[1] // leaves
    first = (lax.axis_index("leaf") * leaves).astype(jnp.int32).reshape(1)
    before = shifted(near_pairs, "leaf", 1)
    window, turned, descent = exchange(
        points, leaf_order, direction, skeleton_basis, transfers, couplings, leaf
    )
    image, sums = near_and_image(
        near_pairs, before, first, turned, window, descent, skeleton_basis, direction, residual,
        points.shape[0],
    )
    factors = reduce(sums)
    return tuple(update(factors, solution, residual, direction, image))


def solution(mesh):
    in_specs = (
        P(None, "leaf"),
        P("leaf"),
        P("leaf", None),
        P(None, "leaf"),
        P(None, "leaf"),
        P(None, "leaf"),
        P(None, "leaf"),
        P("leaf", None, None),
        P(),
    )
    out_specs = (P(None, "leaf"), P(None, "leaf"), P(None, "leaf"))
    return jax.shard_map(local, mesh=mesh, in_specs=in_specs, out_specs=out_specs, check_vma=False)
```

```python
import functools

import jax
import jax.numpy as jnp
from jax import lax
from jax.experimental import pallas as pl
from jax.experimental.pallas import tpu as pltpu
from jax.sharding import PartitionSpec as P

SHARPNESS = 2.0
EPSILON = 1e-06
HIGHEST = lax.Precision.HIGHEST
MESH = pl.DeviceIdType.MESH
LANES = 128
EXTRA = 16
GROUP = 8
VMEM_LIMIT = 56 * 1024 * 1024
NT = (((1,), (1,)), ((), ()))


def shifted(x, axis, by):
    peers = lax.axis_size(axis)
    return lax.ppermute(x, axis, [(i, (i + by) % peers) for i in range(peers)])


def f32_dot(a, b):
    return jnp.dot(a, b, precision=HIGHEST, preferred_element_type=jnp.float32)


def f32_dot_nt(a, b):
    return lax.dot_general(a, b, NT, precision=HIGHEST, preferred_element_type=jnp.float32)


def exchange_kernel(
    count, leaf, points_ref, order_ref, direction_ref, basis_ref, transfers_hbm, couplings_hbm,
    window_ref, turned_ref, descent_ref, tall, transfers, couplings, skel, cur, arrived, coupled,
    load_sem, own_send, own_recv, stage_send, stage_recv, swap_send, swap_recv,
):
    coords, slab = points_ref.shape
    rhs = direction_ref.shape[0]
    depth = transfers.shape[0]
    bits = count.bit_length() - 1
    leaves = slab // leaf
    chunks = slab // LANES
    half = rhs // 2
    me = lax.axis_index("leaf")
    load_t = pltpu.make_async_copy(transfers_hbm, transfers, load_sem.at[0])
    load_c = pltpu.make_async_copy(couplings_hbm, couplings, load_sem.at[1])
    load_t.start()
    load_c.start()
    after, prior = (me + 1) % count, (me + count - 1) % count
    peers = [me + (1 << b) * (1 - 2 * ((me // (1 << b)) % 2)) for b in range(bits)]
    barrier = pltpu.get_barrier_semaphore()
    for peer in [after, prior] + peers:
        pl.semaphore_signal(barrier, inc=1, device_id=(peer,), device_id_type=MESH)

    value = lax.dot_general(
        direction_ref[...].astype(jnp.bfloat16),
        basis_ref[...],
        NT,
        preferred_element_type=jnp.float32,
    )
    skel[0] = value
    load_t.wait()
    for k in range(depth):
        value = f32_dot(value, transfers[k])
        skel[k + 1] = value
    pl.semaphore_wait(barrier, 2 + bits)

    mine = pl.multiple_of((me % 2) * half, half)
    other = pl.multiple_of((1 - me % 2) * half, half)

    def stage(b):
        low = min(b, depth)
        return pltpu.make_async_remote_copy(
            src_ref=skel.at[:, pl.ds(other, half)] if b == 0 else cur.at[pl.ds(low, depth + 1 - low)],
            dst_ref=arrived.at[b, pl.ds(low, depth + 1 - low)],
            send_sem=stage_send.at[b],
            recv_sem=stage_recv.at[b],
            device_id=(peers[b],),
            device_id_type=MESH,
        )

    def place(j, slot):
        return pl.ds(pl.multiple_of(slot * slab + j * leaf, leaf), leaf)

    def to_prior(j):
        return pltpu.make_async_remote_copy(
            src_ref=window_ref.at[:, place(j, 1)],
            dst_ref=window_ref.at[:, place(j, 2)],
            send_sem=own_send.at[0, j],
            recv_sem=own_recv.at[0, j],
            device_id=(prior,),
            device_id_type=MESH,
        )

    def to_after(j):
        return pltpu.make_async_remote_copy(
            src_ref=window_ref.at[:, place(j, 1)],
            dst_ref=window_ref.at[:, place(j, 0)],
            send_sem=own_send.at[1, j],
            recv_sem=own_recv.at[1, j],
            device_id=(after,),
            device_id_type=MESH,
        )

    def arrange(j, carry):
        cols = pl.ds(pl.multiple_of(j * leaf, leaf), leaf)
        order = order_ref[:, cols]
        high = order // LANES
        low = order - high * LANES
        rows = lax.broadcasted_iota(jnp.int32, (LANES, leaf), 0)
        onehot = jnp.where(rows == low, 1.0, 0.0).astype(jnp.bfloat16)
        picked = jnp.zeros((coords, leaf), jnp.float32)
        step = 4
        for c in range(0, chunks, step):
            part = jnp.dot(
                tall[c * coords : (c + step) * coords, :], onehot, preferred_element_type=jnp.float32
            )
            for h in range(step):
                picked = jnp.where(high == c + h, part[h * coords : (h + 1) * coords], picked)
        square = -0.5 * jnp.sum(picked * picked, axis=0, keepdims=True)
        first = square.astype(jnp.bfloat16).astype(jnp.float32)
        second = (square - first).astype(jnp.bfloat16).astype(jnp.float32)
        third = (square - first - second).astype(jnp.bfloat16).astype(jnp.float32)

        def extra(height, at_parts, at_ones):
            row = lax.broadcasted_iota(jnp.int32, (height, leaf), 0)
            out = jnp.where((row >= at_ones) & (row < at_ones + 3), 1.0, 0.0)
            for i, piece in enumerate((first, second, third)):
                out = jnp.where(row == at_parts + i, piece, out)
            return out

        here = place(j, 1)
        window_ref[0:coords, here] = picked.astype(jnp.bfloat16)
        window_ref[coords : coords + EXTRA, here] = extra(EXTRA, 0, 3).astype(jnp.bfloat16)
        window_ref[coords + EXTRA :, here] = direction_ref[:, cols].astype(jnp.bfloat16)

        wide = jnp.concatenate([picked, extra(LANES - coords, 3, 0)], axis=0)
        turned_ref[cols, :] = (2.0 * SHARPNESS * wide.T).astype(jnp.bfloat16)
        return carry

    def send(j, carry):
        @pl.when(me > 0)
        def _():
            to_prior(j).start()

        @pl.when(me < count - 1)
        def _():
            to_after(j).start()

        return carry

    def swap(k):
        return pltpu.make_async_remote_copy(
            src_ref=coupled.at[k, me % 2],
            dst_ref=coupled.at[k, me % 2],
            send_sem=swap_send.at[k],
            recv_sem=swap_recv.at[k],
            device_id=(peers[0],),
            device_id_type=MESH,
        )

    def couple(k):
        coupled[k, me % 2] = f32_dot_nt(f32_dot(cur[k], couplings[k]), couplings[k])
        swap(k).start()

    def both_halves(k):
        swap(k).wait()
        return coupled[k].reshape(rhs, coupled.shape[-1])

    stage(0).start()
    for h in range(chunks):
        tall[h * coords : (h + 1) * coords, :] = points_ref[:, h * LANES : (h + 1) * LANES]
    done = 0
    for b in range(bits):
        upto = min(leaves, -(-leaves * (b + 1) // 2))
        if upto > done:
            lax.fori_loop(done, upto, arrange, 0)
        done = upto
        stage(b).wait()
        low = min(b, depth)
        if b == 0:
            cur[...] = skel[:, pl.ds(mine, half)] + arrived[0]
        else:
            cur[low:] = cur[low:] + arrived[b, low:]
        if b + 1 < bits:
            stage(b + 1).start()
        if b == 1:
            lax.fori_loop(0, leaves, send, 0)
        if b == 0:
            load_c.wait()
        if b < depth:
            couple(b)
    couple(depth)
    descent = both_halves(depth)
    for k in reversed(range(depth)):
        descent = f32_dot_nt(descent, transfers[k]) + both_halves(k)
    descent_ref[...] = descent.astype(jnp.bfloat16)

    def finish(j, carry):
        @pl.when(me > 0)
        def _():
            to_prior(j).wait_send()
            to_after(j).wait_recv()

        @pl.when(me < count - 1)
        def _():
            to_after(j).wait_send()
            to_prior(j).wait_recv()

        return carry

    lax.fori_loop(0, leaves, finish, 0)


def exchange(points, leaf_order, direction, basis, transfers, couplings, leaf):
    count = lax.axis_size("leaf")
    bits = count.bit_length() - 1
    coords, slab = points.shape
    rhs = direction.shape[0]
    depth, rank = transfers.shape[:2]
    leaves = slab // leaf
    height = coords + EXTRA + rhs
    vmem = pl.BlockSpec(memory_space=pltpu.VMEM)
    hbm = pl.BlockSpec(memory_space=pl.ANY)
    half = (depth + 1, rhs // 2, rank)
    return pl.pallas_call(
        functools.partial(exchange_kernel, count, leaf),
        in_specs=[vmem] * 4 + [hbm] * 2,
        out_specs=[vmem] * 3,
        out_shape=[
            jax.ShapeDtypeStruct((height, 3 * slab), jnp.bfloat16),
            jax.ShapeDtypeStruct((slab, LANES), jnp.bfloat16),
            jax.ShapeDtypeStruct((rhs, rank), jnp.bfloat16),
        ],
        scratch_shapes=[
            pltpu.VMEM((slab // LANES * coords, LANES), jnp.bfloat16),
            pltpu.VMEM(transfers.shape, jnp.float32),
            pltpu.VMEM(couplings.shape, jnp.float32),
            pltpu.VMEM((depth + 1, rhs, rank), jnp.float32),
            pltpu.VMEM(half, jnp.float32),
            pltpu.VMEM((bits,) + half, jnp.float32),
            pltpu.VMEM((depth + 1, 2, rhs // 2, rank), jnp.float32),
            pltpu.SemaphoreType.DMA((2,)),
            pltpu.SemaphoreType.DMA((2, leaves)),
            pltpu.SemaphoreType.DMA((2, leaves)),
            pltpu.SemaphoreType.DMA((bits,)),
            pltpu.SemaphoreType.DMA((bits,)),
            pltpu.SemaphoreType.DMA((depth + 1,)),
            pltpu.SemaphoreType.DMA((depth + 1,)),
        ],
        compiler_params=pltpu.CompilerParams(
            vmem_limit_bytes=VMEM_LIMIT, collective_id=1, has_side_effects=True
        ),
        cost_estimate=pl.CostEstimate(
            flops=2 * coords * slab * slab, bytes_accessed=10 << 20, transcendentals=0
        ),
        name="exchange",
    )(points, leaf_order.reshape(1, slab), direction, basis, transfers, couplings)


def near_kernel(
    coords, lists, before, first_ref, turned, window, descent, basis, direction, residual,
    image_ref, sums_ref, acc, slots,
):
    leaves, partners = lists.shape
    leaf = turned.shape[0]
    rhs = direction.shape[0]
    deep = coords + EXTRA
    target = pl.program_id(0)
    whole_id = first_ref[0] + target

    def lists_me(ref, row):
        found = ref[row, 0] == whole_id
        for m in range(1, partners):
            found = found | (ref[row, m] == whole_id)
        return found

    known = jnp.int32(0)
    for m in range(partners):
        slots[known] = lists[target, m] - first_ref[0] + leaves
        known += jnp.where(lists[target, m] >= 0, 1, 0)
    for ref, at in ((lists, leaves), (before, 0)):
        for a in range(leaves):
            slots[known] = a + at
            known += jnp.where(lists_me(ref, a), 1, 0)
    slots[known] = target + leaves
    slots[known + 1] = target + leaves
    acc[...] = jnp.zeros_like(acc)
    rows = leaf

    def two(i, carry):
        cols, weights = [], []
        for s in range(2):
            at = 2 * i + s
            cols.append(pl.ds(pl.multiple_of(slots[at] * leaf, leaf), leaf))
            weight = jnp.where(at < known, 1, jnp.where(at == known, 1 + known, 0))
            weights.append(weight.astype(jnp.float32))
        for r in range(0, leaf, rows):
            total = acc[r : r + rows, :]
            for col, weight in zip(cols, weights):
                exponent = jnp.dot(
                    turned[r : r + rows, 0:deep],
                    window[0:deep, col],
                    preferred_element_type=jnp.float32,
                )
                tile = jnp.exp(exponent).astype(jnp.bfloat16)
                total += weight * lax.dot_general(
                    tile, window[deep:, col], NT, preferred_element_type=jnp.float32
                )
            acc[r : r + rows, :] = total
        return carry

    lax.fori_loop(0, (known + 2) // 2, two, 0)
    d = direction[...]
    r = residual[...]
    image = d + acc[...].T + jnp.dot(descent[...], basis[...], preferred_element_type=jnp.float32)
    image_ref[...] = image

    @pl.when(target == 0)
    def _():
        sums_ref[...] = jnp.zeros_like(sums_ref)

    for q, (x, y) in enumerate(((r, r), (d, image), (r, image), (image, image))):
        both = x * y
        sums_ref[q] += sum(both[:, i : i + LANES] for i in range(0, leaf, LANES))


def near_and_image(lists, before, first, turned, window, descent, basis, direction, residual, coords):
    leaves, partners = lists.shape
    rhs, slab = direction.shape
    rank = basis.shape[0]
    leaf = slab // leaves
    smem = pl.BlockSpec(memory_space=pltpu.SMEM)
    vmem = pl.BlockSpec(memory_space=pltpu.VMEM)
    block = pl.BlockSpec((rhs, leaf), lambda j: (0, j))
    return pl.pallas_call(
        functools.partial(near_kernel, coords),
        grid=(leaves,),
        in_specs=[
            smem, smem, smem,
            pl.BlockSpec((leaf, LANES), lambda j: (j, 0)),
            vmem, vmem,
            pl.BlockSpec((rank, leaf), lambda j: (0, j)),
            block, block,
        ],
        out_specs=[block, pl.BlockSpec((4, rhs, LANES), lambda j: (0, 0, 0))],
        out_shape=[
            jax.ShapeDtypeStruct((rhs, slab), jnp.float32),
            jax.ShapeDtypeStruct((4, rhs, LANES), jnp.float32),
        ],
        scratch_shapes=[
            pltpu.VMEM((leaf, rhs), jnp.float32),
            pltpu.SMEM((partners + 2 * leaves + 2,), jnp.int32),
        ],
        compiler_params=pltpu.CompilerParams(vmem_limit_bytes=VMEM_LIMIT),
        name="near",
    )(lists, before, first, turned, window, descent, basis, direction, residual)


def reduce_kernel(
    count, sums_ref, factors_ref, tall, inner, outer, send_in, recv_in, send_out, recv_out
):
    me = lax.axis_index("leaf")
    groups = count // GROUP
    base = (me // GROUP) * GROUP
    in_peers = [base + (me - base + d) % GROUP for d in range(1, GROUP)]
    out_peers = [(me + GROUP * e) % count for e in range(1, groups)]
    barrier = pltpu.get_barrier_semaphore()
    for peer in in_peers + out_peers:
        pl.semaphore_signal(barrier, inc=1, device_id=(peer,), device_id_type=MESH)

    rhs = sums_ref.shape[1]
    sums = [sums_ref[q] for q in range(4)]
    zero = jnp.zeros((rhs, LANES), jnp.float32)
    lane = lax.broadcasted_iota(jnp.int32, (rhs, LANES), 1)
    packed = zero
    for i, s in enumerate(sums):
        packed = jnp.where(lane == i, jnp.sum(s, axis=1, keepdims=True), packed)
    tall[...] = jnp.zeros_like(tall)
    tall[0:rhs, :] = packed
    inner[0] = tall[...].T[0:8, :]

    pl.semaphore_wait(barrier, len(in_peers) + len(out_peers))

    def all_sum(buffer, peers, send, recv):
        copies = []
        for i, peer in enumerate(peers):
            copy = pltpu.make_async_remote_copy(
                src_ref=buffer.at[0],
                dst_ref=buffer.at[i + 1],
                send_sem=send.at[i],
                recv_sem=recv.at[i],
                device_id=(peer,),
                device_id_type=MESH,
            )
            copy.start()
            copies.append(copy)
        for copy in copies:
            copy.wait()
        total = buffer[0]
        for i in range(len(peers)):
            total = total + buffer[i + 1]
        return total

    total = all_sum(inner, in_peers, send_in, recv_in)
    if groups > 1:
        outer[0] = total
        total = all_sum(outer, out_peers, send_out, recv_out)
    old = total[0:1]
    step = old / (total[1:2] + EPSILON)
    new = jnp.maximum(old - 2.0 * step * total[2:3] + step * step * total[3:4], 0.0)
    ratio = new / (old + EPSILON)
    row = lax.broadcasted_iota(jnp.int32, (LANES, LANES), 0)
    both = jnp.where(row == 0, step, jnp.where(row == 1, ratio, 0.0))
    factors_ref[...] = both.T[0:rhs, :]


def reduce(sums):
    count = lax.axis_size("leaf")
    groups = count // GROUP
    rhs = sums.shape[1]
    vmem = pl.BlockSpec(memory_space=pltpu.VMEM)
    return pl.pallas_call(
        functools.partial(reduce_kernel, count),
        in_specs=[vmem],
        out_specs=vmem,
        out_shape=jax.ShapeDtypeStruct((rhs, LANES), jnp.float32),
        scratch_shapes=[
            pltpu.VMEM((LANES, LANES), jnp.float32),
            pltpu.VMEM((GROUP, 8, LANES), jnp.float32),
            pltpu.VMEM((max(groups, 2), 8, LANES), jnp.float32),
            pltpu.SemaphoreType.DMA((GROUP - 1,)),
            pltpu.SemaphoreType.DMA((GROUP - 1,)),
            pltpu.SemaphoreType.DMA((max(groups - 1, 1),)),
            pltpu.SemaphoreType.DMA((max(groups - 1, 1),)),
        ],
        compiler_params=pltpu.CompilerParams(
            vmem_limit_bytes=VMEM_LIMIT, collective_id=0, has_side_effects=True
        ),
        name="reduce",
    )(sums)


def update_kernel(factors, solution, residual, direction, image, new_solution, new_residual, new_direction):
    step = factors[:, 0:1]
    ratio = factors[:, 1:2]
    d = direction[...]
    new_solution[...] = solution[...] + step * d
    r = residual[...] - step * image[...]
    new_residual[...] = r
    new_direction[...] = r + ratio * d


def update(factors, solution, residual, direction, image):
    rhs, slab = direction.shape
    height = rhs // 4
    block = pl.BlockSpec((height, slab), lambda j: (j, 0))
    shape = jax.ShapeDtypeStruct((rhs, slab), jnp.float32)
    return pl.pallas_call(
        update_kernel,
        grid=(rhs // height,),
        in_specs=[pl.BlockSpec((height, LANES), lambda j: (j, 0))] + [block] * 4,
        out_specs=[block] * 3,
        out_shape=[shape] * 3,
        compiler_params=pltpu.CompilerParams(vmem_limit_bytes=VMEM_LIMIT),
        name="update",
    )(factors, solution, residual, direction, image)


def local(
    points, leaf_order, near_pairs, solution, residual, direction, skeleton_basis, transfers, couplings
):
    leaves = near_pairs.shape[0]
    leaf = points.shape[1] // leaves
    first = (lax.axis_index("leaf") * leaves).astype(jnp.int32).reshape(1)
    before = shifted(near_pairs, "leaf", 1)
    window, turned, descent = exchange(
        points, leaf_order, direction, skeleton_basis, transfers, couplings, leaf
    )
    image, sums = near_and_image(
        near_pairs, before, first, turned, window, descent, skeleton_basis, direction, residual,
        points.shape[0],
    )
    factors = reduce(sums)
    return tuple(update(factors, solution, residual, direction, image))


def solution(mesh):
    in_specs = (
        P(None, "leaf"),
        P("leaf"),
        P("leaf", None),
        P(None, "leaf"),
        P(None, "leaf"),
        P(None, "leaf"),
        P(None, "leaf"),
        P("leaf", None, None),
        P(),
    )
    out_specs = (P(None, "leaf"), P(None, "leaf"), P(None, "leaf"))
    return jax.shard_map(local, mesh=mesh, in_specs=in_specs, out_specs=out_specs, check_vma=False)
```
